32 devices in a mesh: groups: 2 (over y), shard: 4 (over z), sub: 4 (over x, core).
Axes of the slice: x: 2, y: 2, z: 4, core: 2. Of those that a mesh axis runs over, the one named last changes fastest.
Arguments:
- queries: bfloat16 [512, 32, 128], P(('groups', 'shard', 'sub')), parts along dimension 0, may hold values from -6 to 6
- passages: bfloat16 [8192, 64, 128], P(('groups', 'shard', 'sub')), parts along dimension 0, may hold values from -0.5 to 0.5
- pass_len: int32 [8192], P(('groups', 'shard', 'sub')), parts along dimension 0, may hold values from 1 to 64
- owners: int32 [512, 8], P(('groups', 'shard', 'sub')), parts along dimension 0, may hold values from 0 to 15, all different within a row; in each aligned block of 16 rows (0 to 15, 16 to 31, ...) at most 16 rows name the same one
- candidates: int32 [512, 8, 16], P(('groups', 'shard', 'sub')), parts along dimension 0, may hold values from 0 to 255
Outputs:
- scores: float32 [512, 8, 16], P(('groups', 'shard', 'sub')), parts along dimension 0
The draws below stay inside these ranges and needn't reach their ends.
There are 2 independent parts, one for each index of `groups`. The reference program is written for one: setup_inputs(seed, part) draws one part's arguments, and reference() takes and returns one part's arrays. A program takes and returns all parts, laid end to end along the dimension named above; each array names one. Nothing has to cross between parts.
Inputs may be any that keep to these rules, and one draw needn't show every extreme that they name: Each query's 8 owners are distinct; among the 16 queries of one device no owner is named more than 16 times, a bound that some block reaches.
All inputs are finite; a program needn't handle non-finite values.
Results may differ from the reference program's by a relative error of at most 0.0003.
Values may be sent and summed in bfloat16 or wider, within the bound.
A program may use at most 64 MiB of HBM per device.

```python
import math
import jax
import jax.numpy as jnp
import numpy as np
from jax import lax

DIM = 128
LQ = 32
LP = 64
R = 8
KO = 16
Q_DEV = 16
P_DEV = 256
OWNERS = 16
CAP = 16
NQ = 256
NP = 4096


def plant(result, rng, smallest, high):
    longest = result.shape.index(max(result.shape))
    spots = []
    for shift in (0, 1):
        where = [jax.random.randint(jax.random.fold_in(rng, axis), (), 0, length) for axis, length in enumerate(result.shape)]
        where[longest] = (where[longest] + shift) % result.shape[longest]
        spots.append(tuple(where))
    return result.at[spots[0]].set(smallest).at[spots[1]].set(high)


def levels(key, extent, shards, smallest, top_value):
    def one(position, blocks):
        heights = jax.random.uniform(jax.random.fold_in(jax.random.fold_in(key, 6), position), (blocks,), jnp.float32, smallest / len(shards), top_value / len(shards))
        return jnp.repeat(jnp.exp(heights), extent[position] // blocks).reshape((-1,) + (1,) * (len(extent) - position - 1))

    gain = one(*shards[0])
    for cut in shards[1:]:
        gain = gain * one(*cut)
    return gain


def deal_out(rng, own, number, rows, count, top, limit, lean):
    ranking = jax.random.permutation(rng, count)
    heavy_load, ordinary = portions_of(count, rows * top, limit, lean, True), portions_of(count, rows * top, limit, lean, False)
    places = jnp.arange(count)

    def named(tallies, turn):
        used = int((tallies > 0).sum())
        fixed = max(1, used // 4)
        shifted = fixed + (places - fixed + turn * (used - fixed)) % max(1, count - fixed)
        return jnp.zeros((count,), jnp.int32).at[ranking[jnp.where(places < fixed, places, shifted)]].set(jnp.asarray(tallies, jnp.int32))

    tallies = jnp.where(number % 4 == 0, named(heavy_load, number // 4), named(ordinary, number - number // 4 - 1))
    mixed = jax.random.permutation(jax.random.fold_in(own, 3), count)
    giver, receiver = mixed[0:count // 2 * 2:2], mixed[1:count // 2 * 2:2]
    slack = jnp.minimum(tallies[giver] - 1, limit - tallies[receiver]) // 2
    slack = jnp.where((giver == ranking[0]) | (receiver == ranking[0]) | (tallies[receiver] == 0), 0, jnp.maximum(slack, 0))
    shifted = jax.random.randint(jax.random.fold_in(own, 4), (count // 2,), 0, 1 << 20) % (slack + 1)
    tallies = tallies.at[giver].add(-shifted).at[receiver].add(shifted)
    items = jnp.searchsorted(jnp.cumsum(tallies), jnp.arange(rows * top), side="right").astype(jnp.int32)
    table = items.reshape(top, rows).T
    table = table[jax.random.permutation(jax.random.fold_in(own, 1), rows)]
    turn = jax.random.randint(jax.random.fold_in(own, 2), (rows, 1), 0, top)
    return jnp.take_along_axis(table, (jnp.arange(top)[None, :] + turn) % top, axis=1)


def portions_of(amount, total, most, skew, full):
    weights = [(1 << 20) // math.isqrt(rank ** skew) + 1 for rank in range(1, amount + 1)]
    largest = most if full else min(most, max(-(-total // amount), total * weights[0] // sum(weights)))
    least = 1 if total - largest >= amount - 1 else 0
    counts, surplus = [largest] + [least] * (amount - 1), total - largest - least * (amount - 1)
    while surplus > 0:
        free = [i for i in range(1, amount) if counts[i] < largest] or [i for i in range(1, amount) if counts[i] < most]
        whole, remaining = sum([weights[i] for i in free]), surplus
        for i in free:
            more = min(most - counts[i], max(1, remaining * weights[i] // whole), surplus)
            counts[i] = counts[i] + more
            surplus = surplus - more
    return np.array(counts)


def normal_values(own_key, extent, scale, most, split=(), kind=jnp.bfloat16):
    loudness = levels(own_key, extent, split, -0.22, 0.18) if split else 1.0
    drawn = jax.random.normal(own_key, extent, jnp.float32) * scale * loudness
    return jnp.minimum(jnp.maximum(drawn, -most), most).astype(kind)


def setup_inputs(seed: int = 0, part: int = 0) -> dict:
    key_list = jax.random.split(jax.random.key(seed), 6)
    part_keys = jax.random.split(jax.random.fold_in(key_list[5], part), 6)
    queries = normal_values(part_keys[0], (NQ, LQ, DIM), 1.0, 6.0, ((0, 16),))
    passages = normal_values(part_keys[1], (NP, LP, DIM), DIM ** -0.5, 0.5, ((0, 16),))
    pass_len = plant(jax.random.randint(part_keys[2], (NP,), 1, LP + 1), jax.random.fold_in(part_keys[2], 1), 1, LP).astype(jnp.int32)
    owners_keys = jax.random.split(jax.random.fold_in(part_keys[3], 1), NQ // Q_DEV)
    owners_turns = jax.random.permutation(jax.random.fold_in(part_keys[3], 3), NQ // Q_DEV)
    owners = jax.vmap(lambda own, number: deal_out(jax.random.fold_in(part_keys[3], 2), own, number, Q_DEV, OWNERS, R, CAP, 2))(owners_keys, owners_turns).reshape((NQ, R))
    candidates = plant(jax.random.randint(part_keys[4], (NQ, R, KO), 0, P_DEV), jax.random.fold_in(part_keys[4], 1), 0, P_DEV - 1).astype(jnp.int32)
    return dict(queries=queries, passages=passages, pass_len=pass_len, owners=owners, candidates=candidates)


def reference(queries, passages, pass_len, owners, candidates):
    global_ids = (owners[:, :, None] * P_DEV + candidates).astype(jnp.int32)

    def one_query(pair):
        query_tok, query_ids = pair
        flat_ids = query_ids.reshape(-1)
        passage_rows = passages[flat_ids].astype(jnp.float32)
        similar = jnp.einsum("id,kjd->kij", query_tok.astype(jnp.float32), passage_rows)
        slot_pos = jnp.arange(LP, dtype=jnp.int32)
        valid_mask = slot_pos[None, :] < pass_len[flat_ids][:, None]
        similar = jnp.where(valid_mask[:, None, :], similar, -jnp.inf)
        maxima = jnp.max(similar, axis=-1)
        return jnp.mean(maxima, axis=-1).reshape(query_ids.shape)

    return lax.map(one_query, (queries, global_ids))
```

```python
import jax
import jax.numpy as jnp
from jax import lax
from jax.experimental import pallas as pl
from jax.experimental.pallas import tpu as pltpu
from jax.sharding import PartitionSpec as P

AXES = ("shard", "sub")


def score_kernel(route_ref, cand_ref, q_ref, passages_ref, out_ref, maxima, live):
    slots, query_len, feature = q_ref.shape
    tokens = passages_ref.shape[1]
    cand_count = out_ref.shape[1]
    groups = cand_count // 2
    maxima[...] = jnp.zeros_like(maxima)

    def collect(slot, count):
        live[count] = slot
        return count + (route_ref[0, 0, slot] >= 0).astype(jnp.int32)

    count = lax.fori_loop(0, slots, collect, jnp.int32(0), unroll=8)
    live[count] = live[jnp.maximum(count - 1, 0)]
    blank = jnp.zeros((query_len, feature), jnp.bfloat16)

    def one(slot):
        base = route_ref[0, 0, slot] * cand_count
        tok = q_ref[slot]
        weights = jnp.concatenate(
            [jnp.concatenate([tok, blank], 1), jnp.concatenate([blank, tok], 1)], 0
        )
        rows = [passages_ref[cand_ref[slot, base + k]] for k in range(cand_count)]
        left = jnp.concatenate(rows[:groups], 0)
        right = jnp.concatenate(rows[groups:], 0)
        similar = lax.dot_general(
            jnp.concatenate([left, right], 1),
            weights,
            (((1,), (1,)), ((), ())),
            preferred_element_type=jnp.float32,
        )
        for g in range(groups):
            best = jnp.max(similar[g * tokens : (g + 1) * tokens], axis=0, keepdims=True)
            maxima[g, pl.ds(slot, 1), :] = best

    def pair(step, carry):
        one(live[2 * step])
        one(live[2 * step + 1])
        return carry

    lax.fori_loop(0, (count + 1) // 2, pair, 0)

    width = 2 * query_len
    lane = lax.broadcasted_iota(jnp.int32, (width, cand_count), 0)
    column = lax.broadcasted_iota(jnp.int32, (width, cand_count), 1)
    total = jnp.zeros((slots, cand_count), jnp.float32)
    for g in range(groups):
        pick = column == g + groups * (lane >= query_len).astype(jnp.int32)
        pick = pick.astype(jnp.float32).astype(jnp.bfloat16)
        value = maxima[g]
        for _ in range(3):
            part = value.astype(jnp.bfloat16)
            total = total + jnp.dot(part, pick, preferred_element_type=jnp.float32)
            value = value - part.astype(jnp.float32)
    out_ref[...] = total * (1.0 / query_len)


def score_slots(route, cand, queries, passages):
    slots, query_len, feature = queries.shape
    cand_count = 16
    block = min(slots, 256)
    return pl.pallas_call(
        score_kernel,
        grid=(slots // block,),
        out_shape=jax.ShapeDtypeStruct((slots, cand_count), jnp.float32),
        in_specs=[
            pl.BlockSpec((1, 1, block), lambda i: (i, 0, 0), memory_space=pltpu.SMEM),
            pl.BlockSpec((block, cand.shape[1]), lambda i: (i, 0), memory_space=pltpu.SMEM),
            pl.BlockSpec((block, query_len, feature), lambda i: (i, 0, 0)),
            pl.BlockSpec(passages.shape, lambda i: (0, 0, 0)),
        ],
        out_specs=pl.BlockSpec((block, cand_count), lambda i: (i, 0)),
        scratch_shapes=[
            pltpu.VMEM((cand_count // 2, block, 2 * query_len), jnp.float32),
            pltpu.SMEM((block + 1,), jnp.int32),
        ],
        compiler_params=pltpu.CompilerParams(vmem_limit_bytes=48 << 20),
    )(route.reshape(slots // block, 1, block), cand, queries, passages)


def body(queries, passages, pass_len, owners, candidates):
    owner_count = lax.axis_size("shard") * lax.axis_size("sub")
    me = lax.axis_index(AXES)
    query_count, route_count, cand_count = candidates.shape
    tokens = passages.shape[1]
    slot_pos = lax.broadcasted_iota(jnp.int32, (1, tokens, 1), 1)
    filled = jnp.where(slot_pos < pass_len[:, None, None], passages, passages[:, :1, :])
    all_q = lax.all_gather(queries, AXES, axis=0, tiled=True)
    flat = candidates.reshape(query_count, route_count * cand_count)
    packed = jnp.concatenate([flat, jnp.pad(owners, ((0, 0), (0, 128 - route_count)), constant_values=-1)], axis=1)
    all_ids = lax.all_gather(packed, AXES, axis=0, tiled=True)
    all_cand = all_ids[:, : route_count * cand_count]
    all_owners = all_ids[:, route_count * cand_count : route_count * cand_count + route_count]
    numbers = jnp.arange(1, route_count + 1, dtype=jnp.int32)
    route = jnp.sum(jnp.where(all_owners == me, numbers[None, :], 0), axis=1) - 1
    owned = score_slots(route, all_cand, all_q, filled)
    returned = lax.all_to_all(
        owned.reshape(owner_count, query_count, cand_count), AXES, split_axis=0, concat_axis=0, tiled=True
    )
    hit = owners[None, :, :] == jnp.arange(owner_count, dtype=jnp.int32)[:, None, None]
    return jnp.sum(jnp.where(hit[..., None], returned[:, :, None, :], 0.0), axis=0)


def solution(mesh):
    in_specs = (
        P(("groups", "shard", "sub"), None, None),
        P(("groups", "shard", "sub"), None, None),
        P(("groups", "shard", "sub")),
        P(("groups", "shard", "sub"), None),
        P(("groups", "shard", "sub"), None, None),
    )
    out_specs = P(("groups", "shard", "sub"), None, None)
    return jax.shard_map(body, mesh=mesh, in_specs=in_specs, out_specs=out_specs, check_vma=False)
```

```python
import jax
import jax.numpy as jnp
from jax import lax
from jax.experimental import pallas as pl
from jax.experimental.pallas import tpu as pltpu
from jax.sharding import PartitionSpec as P

def place(peer):
    subs = lax.axis_size("sub")
    return {"shard": peer // subs, "sub": lax.rem(peer, subs)}


def greet(me, count):
    barrier = pltpu.get_barrier_semaphore()

    def signal(off, carry):
        peer = lax.rem(me + off, count)
        pl.semaphore_signal(barrier, inc=1, device_id=place(peer), device_id_type=pl.DeviceIdType.MESH)
        return carry

    lax.fori_loop(1, count, signal, 0)
    pl.semaphore_wait(barrier, count - 1)


def position():
    return lax.axis_index("shard") * lax.axis_size("sub") + lax.axis_index("sub")


def gather_kernel(q_ref, ids_ref, all_q, all_ids, own_sem, q_send, q_recv, ids_send, ids_recv):
    count = ids_ref.shape[0]
    me = position()
    local_q = pltpu.make_async_copy(q_ref, all_q.at[me], own_sem.at[0])
    local_ids = pltpu.make_async_copy(ids_ref.at[me], all_ids.at[me], own_sem.at[1])
    local_q.start()
    local_ids.start()
    greet(me, count)

    def copies(off):
        peer = lax.rem(me + off, count)
        ids = pltpu.make_async_remote_copy(
            src_ref=ids_ref.at[peer],
            dst_ref=all_ids.at[me],
            send_sem=ids_send.at[off],
            recv_sem=ids_recv.at[off],
            device_id=place(peer),
            device_id_type=pl.DeviceIdType.MESH,
        )
        tok = pltpu.make_async_remote_copy(
            src_ref=q_ref,
            dst_ref=all_q.at[me],
            send_sem=q_send.at[off],
            recv_sem=q_recv.at[off],
            device_id=place(peer),
            device_id_type=pl.DeviceIdType.MESH,
        )
        return ids, tok

    def start(off, carry):
        ids, tok = copies(off)
        ids.start()
        tok.start()
        return carry

    def finish(off, carry):
        ids, tok = copies(off)
        ids.wait()
        tok.wait()
        return carry

    lax.fori_loop(1, count, start, 0)
    lax.fori_loop(1, count, finish, 0)
    local_q.wait()
    local_ids.wait()


def gather(queries, ids):
    count = ids.shape[0]
    return pl.pallas_call(
        gather_kernel,
        out_shape=(
            jax.ShapeDtypeStruct((count,) + queries.shape, queries.dtype),
            jax.ShapeDtypeStruct(ids.shape, ids.dtype),
        ),
        in_specs=[pl.BlockSpec(memory_space=pl.ANY)] * 2,
        out_specs=[pl.BlockSpec(memory_space=pl.ANY)] * 2,
        scratch_shapes=[pltpu.SemaphoreType.DMA((2,))] + [pltpu.SemaphoreType.DMA((count,))] * 4,
        compiler_params=pltpu.CompilerParams(collective_id=0, has_side_effects=True),
    )(queries, ids)


def return_kernel(owned_ref, out_ref, own_sem, send, recv):
    count = owned_ref.shape[0]
    me = position()
    local = pltpu.make_async_copy(owned_ref.at[me], out_ref.at[me], own_sem)
    local.start()
    greet(me, count)

    def copy(off):
        peer = lax.rem(me + off, count)
        return pltpu.make_async_remote_copy(
            src_ref=owned_ref.at[peer],
            dst_ref=out_ref.at[me],
            send_sem=send.at[off],
            recv_sem=recv.at[off],
            device_id=place(peer),
            device_id_type=pl.DeviceIdType.MESH,
        )

    def start(off, carry):
        copy(off).start()
        return carry

    def finish(off, carry):
        copy(off).wait()
        return carry

    lax.fori_loop(1, count, start, 0)
    lax.fori_loop(1, count, finish, 0)
    local.wait()


def give_back(owned):
    count = owned.shape[0]
    return pl.pallas_call(
        return_kernel,
        out_shape=jax.ShapeDtypeStruct(owned.shape, owned.dtype),
        in_specs=[pl.BlockSpec(memory_space=pl.ANY)],
        out_specs=pl.BlockSpec(memory_space=pl.ANY),
        scratch_shapes=[pltpu.SemaphoreType.DMA] + [pltpu.SemaphoreType.DMA((count,))] * 2,
        compiler_params=pltpu.CompilerParams(collective_id=1, has_side_effects=True),
    )(owned)


def score_kernel(ids_ref, len_ref, q_ref, passages_ref, out_ref, maxima, filled, live):
    sources, per_source, query_len, feature = q_ref.shape
    slots = sources * per_source
    passage_count, tokens, _ = passages_ref.shape
    cand_count = out_ref.shape[-1]
    groups = cand_count // 2
    maxima[...] = jnp.zeros_like(maxima)

    @pl.when(pl.program_id(0) == 0)
    def _():
        slot_pos = lax.broadcasted_iota(jnp.int32, (tokens, feature), 0)

        def fill(p, carry):
            values = passages_ref[p].astype(jnp.float32)
            values = jnp.where(slot_pos < len_ref[p], values, values[0:1])
            filled[p] = values.astype(jnp.bfloat16)
            return carry

        lax.fori_loop(0, passage_count, fill, 0, unroll=8)

    count = jnp.int32(0)
    for query in range(per_source):

        def collect(source, count, query=query):
            live[count] = source * per_source + query
            return count + (ids_ref[source, per_source, query] >= 0).astype(jnp.int32)

        count = lax.fori_loop(0, sources, collect, count, unroll=True)
    live[count] = live[jnp.maximum(count - 1, 0)]
    blank = jnp.zeros((query_len, feature), jnp.bfloat16)

    def one(slot):
        source, query = slot // per_source, lax.rem(slot, per_source)
        base = ids_ref[source, per_source, query] * cand_count
        tok = q_ref[source, query]
        weights = jnp.concatenate(
            [jnp.concatenate([tok, blank], 1), jnp.concatenate([blank, tok], 1)], 0
        )
        rows = [filled[ids_ref[source, query, base + k]] for k in range(cand_count)]
        left = jnp.concatenate(rows[:groups], 0)
        right = jnp.concatenate(rows[groups:], 0)
        similar = lax.dot_general(
            jnp.concatenate([left, right], 1),
            weights,
            (((1,), (1,)), ((), ())),
            preferred_element_type=jnp.float32,
        )
        for g in range(groups):
            best = jnp.max(similar[g * tokens : (g + 1) * tokens], axis=0, keepdims=True)
            maxima[g, pl.ds(slot, 1), :] = best

    def pair(step, carry):
        one(live[2 * step])
        one(live[2 * step + 1])
        return carry

    lax.fori_loop(0, (count + 1) // 2, pair, 0)

    width = 2 * query_len
    lane = lax.broadcasted_iota(jnp.int32, (width, cand_count), 0)
    column = lax.broadcasted_iota(jnp.int32, (width, cand_count), 1)
    total = jnp.zeros((slots, cand_count), jnp.float32)
    for g in range(groups):
        pick = column == g + groups * (lane >= query_len).astype(jnp.int32)
        pick = pick.astype(jnp.float32).astype(jnp.bfloat16)
        value = maxima[g]
        for _ in range(3):
            part = value.astype(jnp.bfloat16)
            total = total + jnp.dot(part, pick, preferred_element_type=jnp.float32)
            value = value - part.astype(jnp.float32)
    out_ref[...] = (total * (1.0 / query_len)).reshape(out_ref.shape)


def score_slots(ids, pass_len, queries, passages, cand_count):
    count, per_source, query_len, feature = queries.shape
    sources = min(count, 16)
    slots = sources * per_source
    return pl.pallas_call(
        score_kernel,
        grid=(count // sources,),
        out_shape=jax.ShapeDtypeStruct((count, per_source, cand_count), jnp.float32),
        in_specs=[
            pl.BlockSpec((sources,) + ids.shape[1:], lambda i: (i, 0, 0), memory_space=pltpu.SMEM),
            pl.BlockSpec(memory_space=pltpu.SMEM),
            pl.BlockSpec((sources, per_source, query_len, feature), lambda i: (i, 0, 0, 0)),
            pl.BlockSpec(passages.shape, lambda i: (0, 0, 0)),
        ],
        out_specs=pl.BlockSpec((sources, per_source, cand_count), lambda i: (i, 0, 0)),
        scratch_shapes=[
            pltpu.VMEM((cand_count // 2, slots, 2 * query_len), jnp.float32),
            pltpu.VMEM(passages.shape, passages.dtype),
            pltpu.SMEM((slots + 1,), jnp.int32),
        ],
        compiler_params=pltpu.CompilerParams(vmem_limit_bytes=48 << 20),
    )(ids, pass_len, queries, passages)


def body(queries, passages, pass_len, owners, candidates):
    owner_count = lax.axis_size("shard") * lax.axis_size("sub")
    query_count, route_count, cand_count = candidates.shape
    flat = candidates.reshape(query_count, route_count * cand_count)
    owner_ids = jnp.arange(owner_count, dtype=jnp.int32)
    numbers = jnp.arange(1, route_count + 1, dtype=jnp.int32)
    hit = owners[None, :, :] == owner_ids[:, None, None]
    route = jnp.sum(jnp.where(hit, numbers, 0), axis=2) - 1
    route = jnp.pad(route[:, None, :], ((0, 0), (0, 7), (0, flat.shape[1] - query_count)))
    ids = jnp.concatenate([jnp.broadcast_to(flat[None], (owner_count,) + flat.shape), route], axis=1)
    all_q, all_ids = gather(queries, ids)
    returned = give_back(score_slots(all_ids, pass_len, all_q, passages, cand_count))
    return jnp.sum(jnp.where(hit[..., None], returned[:, :, None, :], 0.0), axis=0)


def solution(mesh):
    in_specs = (
        P(("groups", "shard", "sub"), None, None),
        P(("groups", "shard", "sub"), None, None),
        P(("groups", "shard", "sub")),
        P(("groups", "shard", "sub"), None),
        P(("groups", "shard", "sub"), None, None),
    )
    out_specs = P(("groups", "shard", "sub"), None, None)
    return jax.shard_map(body, mesh=mesh, in_specs=in_specs, out_specs=out_specs, check_vma=False)
```

```python
import jax
import jax.numpy as jnp
from jax import lax
from jax.experimental import pallas as pl
from jax.experimental.pallas import tpu as pltpu
from jax.sharding import PartitionSpec as P

def place(peer):
    subs = lax.axis_size("sub")
    return {"shard": peer // subs, "sub": lax.rem(peer, subs)}


def greet(me, count):
    barrier = pltpu.get_barrier_semaphore()

    def signal(off, carry):
        peer = lax.rem(me + off, count)
        pl.semaphore_signal(barrier, inc=1, device_id=place(peer), device_id_type=pl.DeviceIdType.MESH)
        return carry

    lax.fori_loop(1, count, signal, 0)
    pl.semaphore_wait(barrier, count - 1)


def position():
    return lax.axis_index("shard") * lax.axis_size("sub") + lax.axis_index("sub")


def gather_kernel(q_ref, ids_ref, all_q, all_ids, own_sem, z_send, z_recv, x_send, x_recv, c_send, c_recv):
    depth = lax.axis_size("shard")
    subs = lax.axis_size("sub")
    width = subs // 2
    z, s = lax.axis_index("shard"), lax.axis_index("sub")
    x, core = s // 2, lax.rem(s, 2)
    pairs = ((q_ref, all_q), (ids_ref, all_ids))

    def row(block_z, block_x, block_core):
        return block_z * subs + block_x * 2 + block_core

    def along(step, size, at):
        return lax.rem(at + size + step, size)

    across = {"shard": z, "sub": x * 2 + 1 - core}
    z_peers = [{"shard": along(dz, depth, z), "sub": s} for dz in range(depth)]
    x_peers = [{"shard": z, "sub": along(dx, width, x) * 2 + core} for dx in range(width)]
    mesh_ids = pl.DeviceIdType.MESH

    local = [pltpu.make_async_copy(own, every.at[row(z, x, core)], own_sem.at[i]) for i, (own, every) in enumerate(pairs)]
    for copy in local:
        copy.start()
    barrier = pltpu.get_barrier_semaphore()
    for peer in z_peers[1:] + x_peers[1:] + [across]:
        pl.semaphore_signal(barrier, inc=1, device_id=peer, device_id_type=mesh_ids)
    pl.semaphore_wait(barrier, depth + width - 1)

    def send(block, own, peer, send_sem, recv_sem):
        copies = [
            pltpu.make_async_remote_copy(
                src_ref=mine if own else every.at[block],
                dst_ref=every.at[block],
                send_sem=send_sem(i),
                recv_sem=recv_sem(i),
                device_id=peer,
                device_id_type=mesh_ids,
            )
            for i, (mine, every) in enumerate(pairs)
        ]
        for copy in copies:
            copy.start()
        return copies

    by_z, by_x, by_core = {}, {}, []
    for dz in range(1, depth):
        by_z[dz] = send(
            row(z, x, core), True, z_peers[dz], lambda i: z_send.at[i, dz], lambda i: z_recv.at[i, dz]
        )

    def pass_on(dz):
        block = row(along(-dz, depth, z), x, core)
        for dx in range(1, width):
            by_x[dz, dx] = send(
                block, dz == 0, x_peers[dx], lambda i: x_send.at[i, dz, dx], lambda i: x_recv.at[i, dz, dx]
            )
        by_core.extend(send(block, dz == 0, across, lambda i: c_send.at[i, dz, 0], lambda i: c_recv.at[i, dz, 0]))

    def cross(dz):
        for dx in range(1, width):
            for copy in by_x[dz, dx]:
                copy.wait_recv()
            block = row(along(-dz, depth, z), along(-dx, width, x), core)
            by_core.extend(
                send(block, False, across, lambda i: c_send.at[i, dz, dx], lambda i: c_recv.at[i, dz, dx])
            )

    pass_on(0)
    for dz in range(1, depth):
        for copy in by_z[dz]:
            copy.wait_recv()
        pass_on(dz)
    for dz in range(depth):
        cross(dz)
    for copy in by_core:
        copy.wait()
    for copies in list(by_z.values()) + list(by_x.values()):
        for copy in copies:
            copy.wait_send()
    for copy in local:
        copy.wait()


def gather(queries, ids):
    depth, subs = lax.axis_size("shard"), lax.axis_size("sub")
    count = depth * subs
    sem = pltpu.SemaphoreType.DMA
    return pl.pallas_call(
        gather_kernel,
        out_shape=(
            jax.ShapeDtypeStruct((count,) + queries.shape, queries.dtype),
            jax.ShapeDtypeStruct((count,) + ids.shape, ids.dtype),
        ),
        in_specs=[pl.BlockSpec(memory_space=pl.ANY)] * 2,
        out_specs=[pl.BlockSpec(memory_space=pl.ANY)] * 2,
        scratch_shapes=[sem((2,))] + [sem((2, depth))] * 2 + [sem((2, depth, subs // 2))] * 4,
        compiler_params=pltpu.CompilerParams(collective_id=0, has_side_effects=True),
    )(queries, ids)


def return_kernel(owned_ref, out_ref, own_sem, send, recv):
    count = owned_ref.shape[0]
    me = position()
    local = pltpu.make_async_copy(owned_ref.at[me], out_ref.at[me], own_sem)
    local.start()
    greet(me, count)

    def copy(off):
        peer = lax.rem(me + off, count)
        return pltpu.make_async_remote_copy(
            src_ref=owned_ref.at[peer],
            dst_ref=out_ref.at[me],
            send_sem=send.at[off],
            recv_sem=recv.at[off],
            device_id=place(peer),
            device_id_type=pl.DeviceIdType.MESH,
        )

    def start(off, carry):
        copy(off).start()
        return carry

    def finish(off, carry):
        copy(off).wait()
        return carry

    lax.fori_loop(1, count, start, 0)
    lax.fori_loop(1, count, finish, 0)
    local.wait()


def give_back(owned):
    count = owned.shape[0]
    return pl.pallas_call(
        return_kernel,
        out_shape=jax.ShapeDtypeStruct(owned.shape, owned.dtype),
        in_specs=[pl.BlockSpec(memory_space=pl.ANY)],
        out_specs=pl.BlockSpec(memory_space=pl.ANY),
        scratch_shapes=[pltpu.SemaphoreType.DMA] + [pltpu.SemaphoreType.DMA((count,))] * 2,
        compiler_params=pltpu.CompilerParams(collective_id=1, has_side_effects=True),
    )(owned)


def score_kernel(ids_ref, len_ref, q_ref, passages_ref, out_ref, maxima, filled, live, route):
    sources, per_source, query_len, feature = q_ref.shape
    slots = sources * per_source
    passage_count, tokens, _ = passages_ref.shape
    cand_count = out_ref.shape[-1]
    groups = cand_count // 2
    maxima[...] = jnp.zeros_like(maxima)

    @pl.when(pl.program_id(0) == 0)
    def _():
        slot_pos = lax.broadcasted_iota(jnp.int32, (tokens, feature), 0)

        def fill(p, carry):
            values = passages_ref[p].astype(jnp.float32)
            values = jnp.where(slot_pos < len_ref[p], values, values[0:1])
            filled[p] = values.astype(jnp.bfloat16)
            return carry

        lax.fori_loop(0, passage_count, fill, 0, unroll=8)

    me = position()
    routes = ids_ref.shape[2] // per_source

    def collect(slot, count):
        source, query = slot // per_source, lax.rem(slot, per_source)
        found = jnp.int32(-1)
        for r in range(routes):
            found = jnp.where(ids_ref[source, per_source, query * routes + r] == me, r, found)
        route[slot] = found
        live[count] = slot
        return count + (found >= 0).astype(jnp.int32)

    count = lax.fori_loop(0, slots, collect, jnp.int32(0), unroll=4)
    live[count] = live[jnp.maximum(count - 1, 0)]
    blank = jnp.zeros((query_len, feature), jnp.bfloat16)

    def one(slot):
        source, query = slot // per_source, lax.rem(slot, per_source)
        base = route[slot] * cand_count
        tok = q_ref[source, query]
        weights = jnp.concatenate(
            [jnp.concatenate([tok, blank], 1), jnp.concatenate([blank, tok], 1)], 0
        )
        rows = [filled[ids_ref[source, query, base + k]] for k in range(cand_count)]
        left = jnp.concatenate(rows[:groups], 0)
        right = jnp.concatenate(rows[groups:], 0)
        similar = lax.dot_general(
            jnp.concatenate([left, right], 1),
            weights,
            (((1,), (1,)), ((), ())),
            preferred_element_type=jnp.float32,
        )
        for g in range(groups):
            best = jnp.max(similar[g * tokens : (g + 1) * tokens], axis=0, keepdims=True)
            maxima[g, pl.ds(slot, 1), :] = best

    def pair(step, carry):
        one(live[2 * step])
        one(live[2 * step + 1])
        return carry

    lax.fori_loop(0, (count + 1) // 2, pair, 0)

    width = 2 * query_len
    lane = lax.broadcasted_iota(jnp.int32, (width, cand_count), 0)
    column = lax.broadcasted_iota(jnp.int32, (width, cand_count), 1)
    total = jnp.zeros((slots, cand_count), jnp.float32)
    for g in range(groups):
        pick = column == g + groups * (lane >= query_len).astype(jnp.int32)
        pick = pick.astype(jnp.float32).astype(jnp.bfloat16)
        value = maxima[g]
        for _ in range(3):
            part = value.astype(jnp.bfloat16)
            total = total + jnp.dot(part, pick, preferred_element_type=jnp.float32)
            value = value - part.astype(jnp.float32)
    out_ref[...] = (total * (1.0 / query_len)).reshape(out_ref.shape)


def score_slots(ids, pass_len, queries, passages, cand_count):
    count, per_source, query_len, feature = queries.shape
    sources = min(count, 16)
    slots = sources * per_source
    return pl.pallas_call(
        score_kernel,
        grid=(count // sources,),
        out_shape=jax.ShapeDtypeStruct((count, per_source, cand_count), jnp.float32),
        in_specs=[
            pl.BlockSpec((sources,) + ids.shape[1:], lambda i: (i, 0, 0), memory_space=pltpu.SMEM),
            pl.BlockSpec(memory_space=pltpu.SMEM),
            pl.BlockSpec((sources, per_source, query_len, feature), lambda i: (i, 0, 0, 0)),
            pl.BlockSpec(passages.shape, lambda i: (0, 0, 0)),
        ],
        out_specs=pl.BlockSpec((sources, per_source, cand_count), lambda i: (i, 0, 0)),
        scratch_shapes=[
            pltpu.VMEM((cand_count // 2, slots, 2 * query_len), jnp.float32),
            pltpu.VMEM(passages.shape, passages.dtype),
            pltpu.SMEM((slots + 1,), jnp.int32),
            pltpu.SMEM((slots,), jnp.int32),
        ],
        compiler_params=pltpu.CompilerParams(vmem_limit_bytes=48 << 20),
    )(ids, pass_len, queries, passages)


def body(queries, passages, pass_len, owners, candidates):
    owner_count = lax.axis_size("shard") * lax.axis_size("sub")
    query_count, route_count, cand_count = candidates.shape
    flat = candidates.reshape(query_count, route_count * cand_count)
    spare = jnp.zeros((7, flat.shape[1]), jnp.int32)
    ids = jnp.concatenate([flat, owners.reshape(1, query_count * route_count), spare], axis=0)
    all_q, all_ids = gather(queries, ids)
    returned = give_back(score_slots(all_ids, pass_len, all_q, passages, cand_count))
    hit = owners[None, :, :] == jnp.arange(owner_count, dtype=jnp.int32)[:, None, None]
    return jnp.sum(jnp.where(hit[..., None], returned[:, :, None, :], 0.0), axis=0)


def solution(mesh):
    in_specs = (
        P(("groups", "shard", "sub"), None, None),
        P(("groups", "shard", "sub"), None, None),
        P(("groups", "shard", "sub")),
        P(("groups", "shard", "sub"), None),
        P(("groups", "shard", "sub"), None, None),
    )
    out_specs = P(("groups", "shard", "sub"), None, None)
    return jax.shard_map(body, mesh=mesh, in_specs=in_specs, out_specs=out_specs, check_vma=False)
```

```python
import jax
import jax.numpy as jnp
from jax import lax
from jax.experimental import pallas as pl
from jax.experimental.pallas import tpu as pltpu
from jax.sharding import PartitionSpec as P

def place(peer):
    subs = lax.axis_size("sub")
    return {"shard": peer // subs, "sub": lax.rem(peer, subs)}


def greet(me, count):
    barrier = pltpu.get_barrier_semaphore()

    def signal(off, carry):
        peer = lax.rem(me + off, count)
        pl.semaphore_signal(barrier, inc=1, device_id=place(peer), device_id_type=pl.DeviceIdType.MESH)
        return carry

    lax.fori_loop(1, count, signal, 0)
    pl.semaphore_wait(barrier, count - 1)


def position():
    return lax.axis_index("shard") * lax.axis_size("sub") + lax.axis_index("sub")


def gather_kernel(q_ref, ids_ref, all_q, all_ids, own_sem, z_send, z_recv, x_send, x_recv, c_send, c_recv):
    depth = lax.axis_size("shard")
    subs = lax.axis_size("sub")
    width = subs // 2
    z, s = lax.axis_index("shard"), lax.axis_index("sub")
    x, core = s // 2, lax.rem(s, 2)
    pairs = ((q_ref, all_q), (ids_ref, all_ids))

    def row(block_z, block_x, block_core):
        return block_z * subs + block_x * 2 + block_core

    def along(step, size, at):
        return lax.rem(at + size + step, size)

    across = {"shard": z, "sub": x * 2 + 1 - core}
    z_peers = [{"shard": along(dz, depth, z), "sub": s} for dz in range(depth)]
    x_peers = [{"shard": z, "sub": along(dx, width, x) * 2 + core} for dx in range(width)]
    mesh_ids = pl.DeviceIdType.MESH

    local = [pltpu.make_async_copy(own, every.at[row(z, x, core)], own_sem.at[i]) for i, (own, every) in enumerate(pairs)]
    for copy in local:
        copy.start()
    barrier = pltpu.get_barrier_semaphore()
    for peer in z_peers[1:] + x_peers[1:] + [across]:
        pl.semaphore_signal(barrier, inc=1, device_id=peer, device_id_type=mesh_ids)
    pl.semaphore_wait(barrier, depth + width - 1)

    def send(block, own, peer, send_sem, recv_sem):
        copies = [
            pltpu.make_async_remote_copy(
                src_ref=mine if own else every.at[block],
                dst_ref=every.at[block],
                send_sem=send_sem(i),
                recv_sem=recv_sem(i),
                device_id=peer,
                device_id_type=mesh_ids,
            )
            for i, (mine, every) in enumerate(pairs)
        ]
        for copy in copies:
            copy.start()
        return copies

    by_z, by_x, by_core = {}, {}, []
    for dz in range(1, depth):
        by_z[dz] = send(
            row(z, x, core), True, z_peers[dz], lambda i: z_send.at[i, dz], lambda i: z_recv.at[i, dz]
        )

    def pass_on(dz):
        block = row(along(-dz, depth, z), x, core)
        for dx in range(1, width):
            by_x[dz, dx] = send(
                block, dz == 0, x_peers[dx], lambda i: x_send.at[i, dz, dx], lambda i: x_recv.at[i, dz, dx]
            )
        by_core.extend(send(block, dz == 0, across, lambda i: c_send.at[i, dz, 0], lambda i: c_recv.at[i, dz, 0]))

    def cross(dz):
        for dx in range(1, width):
            for copy in by_x[dz, dx]:
                copy.wait_recv()
            block = row(along(-dz, depth, z), along(-dx, width, x), core)
            by_core.extend(
                send(block, False, across, lambda i: c_send.at[i, dz, dx], lambda i: c_recv.at[i, dz, dx])
            )

    pass_on(0)
    for dz in range(1, depth):
        for copy in by_z[dz]:
            copy.wait_recv()
        pass_on(dz)
    for dz in range(depth):
        cross(dz)
    for copy in by_core:
        copy.wait()
    for copies in list(by_z.values()) + list(by_x.values()):
        for copy in copies:
            copy.wait_send()
    for copy in local:
        copy.wait()


def gather(queries, ids):
    depth, subs = lax.axis_size("shard"), lax.axis_size("sub")
    count = depth * subs
    sem = pltpu.SemaphoreType.DMA
    return pl.pallas_call(
        gather_kernel,
        out_shape=(
            jax.ShapeDtypeStruct((count,) + queries.shape, queries.dtype),
            jax.ShapeDtypeStruct((count,) + ids.shape, ids.dtype),
        ),
        in_specs=[pl.BlockSpec(memory_space=pl.ANY)] * 2,
        out_specs=[pl.BlockSpec(memory_space=pl.ANY)] * 2,
        scratch_shapes=[sem((2,))] + [sem((2, depth))] * 2 + [sem((2, depth, subs // 2))] * 4,
        compiler_params=pltpu.CompilerParams(collective_id=0, has_side_effects=True),
    )(queries, ids)


def return_kernel(owned_ref, out_ref, own_sem, send, recv):
    count = owned_ref.shape[0]
    me = position()
    local = pltpu.make_async_copy(owned_ref.at[me], out_ref.at[me], own_sem)
    local.start()
    greet(me, count)

    def copy(off):
        peer = lax.rem(me + off, count)
        return pltpu.make_async_remote_copy(
            src_ref=owned_ref.at[peer],
            dst_ref=out_ref.at[me],
            send_sem=send.at[off],
            recv_sem=recv.at[off],
            device_id=place(peer),
            device_id_type=pl.DeviceIdType.MESH,
        )

    def start(off, carry):
        copy(off).start()
        return carry

    def finish(off, carry):
        copy(off).wait()
        return carry

    lax.fori_loop(1, count, start, 0)
    lax.fori_loop(1, count, finish, 0)
    local.wait()


def give_back(owned):
    count = owned.shape[0]
    return pl.pallas_call(
        return_kernel,
        out_shape=jax.ShapeDtypeStruct(owned.shape, owned.dtype),
        in_specs=[pl.BlockSpec(memory_space=pl.ANY)],
        out_specs=pl.BlockSpec(memory_space=pl.ANY),
        scratch_shapes=[pltpu.SemaphoreType.DMA] + [pltpu.SemaphoreType.DMA((count,))] * 2,
        compiler_params=pltpu.CompilerParams(collective_id=1, has_side_effects=True),
    )(owned)


def score_kernel(route_ref, ids_ref, len_ref, q_ref, passages_ref, out_ref, maxima, filled, live):
    sources, per_source, query_len, feature = q_ref.shape
    slots = sources * per_source
    passage_count, tokens, _ = passages_ref.shape
    cand_count = out_ref.shape[-1]
    groups = cand_count // 2
    maxima[...] = jnp.zeros_like(maxima)

    @pl.when(pl.program_id(0) == 0)
    def _():
        slot_pos = lax.broadcasted_iota(jnp.int32, (tokens, feature), 0)

        def fill(p, carry):
            values = passages_ref[p].astype(jnp.float32)
            values = jnp.where(slot_pos < len_ref[p], values, values[0:1])
            filled[p] = values.astype(jnp.bfloat16)
            return carry

        lax.fori_loop(0, passage_count, fill, 0, unroll=8)

    def collect(slot, count):
        live[count] = slot
        return count + (route_ref[slot // per_source, lax.rem(slot, per_source)] >= 0).astype(jnp.int32)

    count = lax.fori_loop(0, slots, collect, jnp.int32(0), unroll=16)
    live[count] = live[jnp.maximum(count - 1, 0)]
    blank = jnp.zeros((query_len, feature), jnp.bfloat16)

    def one(slot):
        source, query = slot // per_source, lax.rem(slot, per_source)
        base = route_ref[source, query] * cand_count
        tok = q_ref[source, query]
        weights = jnp.concatenate(
            [jnp.concatenate([tok, blank], 1), jnp.concatenate([blank, tok], 1)], 0
        )
        rows = [filled[ids_ref[source, query, base + k]] for k in range(cand_count)]
        left = jnp.concatenate(rows[:groups], 0)
        right = jnp.concatenate(rows[groups:], 0)
        similar = lax.dot_general(
            jnp.concatenate([left, right], 1),
            weights,
            (((1,), (1,)), ((), ())),
            preferred_element_type=jnp.float32,
        )
        for g in range(groups):
            best = jnp.max(similar[g * tokens : (g + 1) * tokens], axis=0, keepdims=True)
            maxima[g, pl.ds(slot, 1), :] = best

    def pair(step, carry):
        one(live[2 * step])
        one(live[2 * step + 1])
        return carry

    lax.fori_loop(0, (count + 1) // 2, pair, 0)

    width = 2 * query_len
    lane = lax.broadcasted_iota(jnp.int32, (width, cand_count), 0)
    column = lax.broadcasted_iota(jnp.int32, (width, cand_count), 1)
    total = jnp.zeros((slots, cand_count), jnp.float32)
    for g in range(groups):
        pick = column == g + groups * (lane >= query_len).astype(jnp.int32)
        pick = pick.astype(jnp.float32).astype(jnp.bfloat16)
        value = maxima[g]
        for _ in range(3):
            part = value.astype(jnp.bfloat16)
            total = total + jnp.dot(part, pick, preferred_element_type=jnp.float32)
            value = value - part.astype(jnp.float32)
    out_ref[...] = (total * (1.0 / query_len)).reshape(out_ref.shape)


def score_slots(route, ids, pass_len, queries, passages, cand_count):
    count, per_source, query_len, feature = queries.shape
    sources = min(count, 16)
    slots = sources * per_source
    return pl.pallas_call(
        score_kernel,
        grid=(count // sources,),
        out_shape=jax.ShapeDtypeStruct((count, per_source, cand_count), jnp.float32),
        in_specs=[
            pl.BlockSpec((sources, per_source), lambda i: (i, 0), memory_space=pltpu.SMEM),
            pl.BlockSpec((sources,) + ids.shape[1:], lambda i: (i, 0, 0), memory_space=pltpu.SMEM),
            pl.BlockSpec(memory_space=pltpu.SMEM),
            pl.BlockSpec((sources, per_source, query_len, feature), lambda i: (i, 0, 0, 0)),
            pl.BlockSpec(passages.shape, lambda i: (0, 0, 0)),
        ],
        out_specs=pl.BlockSpec((sources, per_source, cand_count), lambda i: (i, 0, 0)),
        scratch_shapes=[
            pltpu.VMEM((cand_count // 2, slots, 2 * query_len), jnp.float32),
            pltpu.VMEM(passages.shape, passages.dtype),
            pltpu.SMEM((slots + 1,), jnp.int32),
        ],
        compiler_params=pltpu.CompilerParams(vmem_limit_bytes=48 << 20),
    )(route, ids, pass_len, queries, passages)


def body(queries, passages, pass_len, owners, candidates):
    owner_count = lax.axis_size("shard") * lax.axis_size("sub")
    query_count, route_count, cand_count = candidates.shape
    flat = candidates.reshape(query_count, route_count * cand_count)
    spare = jnp.zeros((7, flat.shape[1]), jnp.int32)
    ids = jnp.concatenate([flat, owners.reshape(1, query_count * route_count), spare], axis=0)
    all_q, all_ids = gather(queries, ids)
    place_in_row = jnp.arange(query_count * route_count, dtype=jnp.int32)
    number = (lax.rem(place_in_row, route_count) + 1).astype(jnp.float32)
    named = jnp.where(all_ids[:, query_count, :] == position(), number[None, :], 0.0)
    fold = place_in_row[:, None] // route_count == jnp.arange(query_count, dtype=jnp.int32)[None, :]
    route = jnp.dot(
        named.astype(jnp.bfloat16), fold.astype(jnp.bfloat16), preferred_element_type=jnp.float32
    ).astype(jnp.int32) - 1
    returned = give_back(score_slots(route, all_ids, pass_len, all_q, passages, cand_count))
    hit = owners[None, :, :] == jnp.arange(owner_count, dtype=jnp.int32)[:, None, None]
    return jnp.sum(jnp.where(hit[..., None], returned[:, :, None, :], 0.0), axis=0)


def solution(mesh):
    in_specs = (
        P(("groups", "shard", "sub"), None, None),
        P(("groups", "shard", "sub"), None, None),
        P(("groups", "shard", "sub")),
        P(("groups", "shard", "sub"), None),
        P(("groups", "shard", "sub"), None, None),
    )
    out_specs = P(("groups", "shard", "sub"), None, None)
    return jax.shard_map(body, mesh=mesh, in_specs=in_specs, out_specs=out_specs, check_vma=False)
```

```python
import jax
import jax.numpy as jnp
from jax import lax
from jax.experimental import pallas as pl
from jax.experimental.pallas import tpu as pltpu
from jax.sharding import PartitionSpec as P

def place(peer):
    subs = lax.axis_size("sub")
    return {"shard": peer // subs, "sub": lax.rem(peer, subs)}


def greet(me, count):
    barrier = pltpu.get_barrier_semaphore()

    def signal(off, carry):
        peer = lax.rem(me + off, count)
        pl.semaphore_signal(barrier, inc=1, device_id=place(peer), device_id_type=pl.DeviceIdType.MESH)
        return carry

    lax.fori_loop(1, count, signal, 0)
    pl.semaphore_wait(barrier, count - 1)


def position():
    return lax.axis_index("shard") * lax.axis_size("sub") + lax.axis_index("sub")


def gather_kernel(q_ref, ids_ref, all_q, all_ids, own_sem, z_send, z_recv, x_send, x_recv, c_send, c_recv):
    depth = lax.axis_size("shard")
    subs = lax.axis_size("sub")
    width = subs // 2
    z, s = lax.axis_index("shard"), lax.axis_index("sub")
    x, core = s // 2, lax.rem(s, 2)
    pairs = ((q_ref, all_q), (ids_ref, all_ids))

    def row(block_z, block_x, block_core):
        return block_z * subs + block_x * 2 + block_core

    def along(step, size, at):
        return lax.rem(at + size + step, size)

    across = {"shard": z, "sub": x * 2 + 1 - core}
    z_peers = [{"shard": along(dz, depth, z), "sub": s} for dz in range(depth)]
    x_peers = [{"shard": z, "sub": along(dx, width, x) * 2 + core} for dx in range(width)]
    mesh_ids = pl.DeviceIdType.MESH

    local = [pltpu.make_async_copy(own, every.at[row(z, x, core)], own_sem.at[i]) for i, (own, every) in enumerate(pairs)]
    for copy in local:
        copy.start()
    barrier = pltpu.get_barrier_semaphore()
    for peer in z_peers[1:] + x_peers[1:] + [across]:
        pl.semaphore_signal(barrier, inc=1, device_id=peer, device_id_type=mesh_ids)
    pl.semaphore_wait(barrier, depth + width - 1)

    def send(block, own, peer, send_sem, recv_sem):
        copies = [
            pltpu.make_async_remote_copy(
                src_ref=mine if own else every.at[block],
                dst_ref=every.at[block],
                send_sem=send_sem(i),
                recv_sem=recv_sem(i),
                device_id=peer,
                device_id_type=mesh_ids,
            )
            for i, (mine, every) in enumerate(pairs)
        ]
        for copy in copies:
            copy.start()
        return copies

    by_z, by_x, by_core = {}, {}, []
    for dz in range(1, depth):
        by_z[dz] = send(
            row(z, x, core), True, z_peers[dz], lambda i: z_send.at[i, dz], lambda i: z_recv.at[i, dz]
        )

    def pass_on(dz):
        block = row(along(-dz, depth, z), x, core)
        for dx in range(1, width):
            by_x[dz, dx] = send(
                block, dz == 0, x_peers[dx], lambda i: x_send.at[i, dz, dx], lambda i: x_recv.at[i, dz, dx]
            )
        by_core.extend(send(block, dz == 0, across, lambda i: c_send.at[i, dz, 0], lambda i: c_recv.at[i, dz, 0]))

    def cross(dz):
        for dx in range(1, width):
            for copy in by_x[dz, dx]:
                copy.wait_recv()
            block = row(along(-dz, depth, z), along(-dx, width, x), core)
            by_core.extend(
                send(block, False, across, lambda i: c_send.at[i, dz, dx], lambda i: c_recv.at[i, dz, dx])
            )

    pass_on(0)
    for dz in range(1, depth):
        for copy in by_z[dz]:
            copy.wait_recv()
        pass_on(dz)
    for dz in range(depth):
        cross(dz)
    for copy in by_core:
        copy.wait()
    for copies in list(by_z.values()) + list(by_x.values()):
        for copy in copies:
            copy.wait_send()
    for copy in local:
        copy.wait()


def gather(queries, ids):
    depth, subs = lax.axis_size("shard"), lax.axis_size("sub")
    count = depth * subs
    sem = pltpu.SemaphoreType.DMA
    return pl.pallas_call(
        gather_kernel,
        out_shape=(
            jax.ShapeDtypeStruct((count,) + queries.shape, queries.dtype),
            jax.ShapeDtypeStruct((count,) + ids.shape, ids.dtype),
        ),
        in_specs=[pl.BlockSpec(memory_space=pl.ANY)] * 2,
        out_specs=[pl.BlockSpec(memory_space=pl.ANY)] * 2,
        scratch_shapes=[sem((2,))] + [sem((2, depth))] * 2 + [sem((2, depth, subs // 2))] * 4,
        compiler_params=pltpu.CompilerParams(collective_id=0, has_side_effects=True),
    )(queries, ids)


def return_kernel(owned_ref, out_ref, own_sem, send, recv):
    count = owned_ref.shape[0]
    me = position()
    local = pltpu.make_async_copy(owned_ref.at[me], out_ref.at[me], own_sem)
    local.start()
    greet(me, count)

    def copy(off):
        peer = lax.rem(me + off, count)
        return pltpu.make_async_remote_copy(
            src_ref=owned_ref.at[peer],
            dst_ref=out_ref.at[me],
            send_sem=send.at[off],
            recv_sem=recv.at[off],
            device_id=place(peer),
            device_id_type=pl.DeviceIdType.MESH,
        )

    def start(off, carry):
        copy(off).start()
        return carry

    def finish(off, carry):
        copy(off).wait()
        return carry

    lax.fori_loop(1, count, start, 0)
    lax.fori_loop(1, count, finish, 0)
    local.wait()


def give_back(owned):
    count = owned.shape[0]
    return pl.pallas_call(
        return_kernel,
        out_shape=jax.ShapeDtypeStruct(owned.shape, owned.dtype),
        in_specs=[pl.BlockSpec(memory_space=pl.ANY)],
        out_specs=pl.BlockSpec(memory_space=pl.ANY),
        scratch_shapes=[pltpu.SemaphoreType.DMA] + [pltpu.SemaphoreType.DMA((count,))] * 2,
        compiler_params=pltpu.CompilerParams(collective_id=1, has_side_effects=True),
    )(owned)


def score_kernel(route_ref, ids_ref, len_ref, q_ref, passages_ref, out_ref, maxima, filled, live):
    sources, per_source, query_len, feature = q_ref.shape
    slots = sources * per_source
    passage_count, tokens, _ = passages_ref.shape
    cand_count = out_ref.shape[-1]
    groups = cand_count // 2
    maxima[...] = jnp.zeros_like(maxima)

    @pl.when(pl.program_id(0) == 0)
    def _():
        slot_pos = lax.broadcasted_iota(jnp.int32, (tokens, feature), 0)

        def fill(p, carry):
            values = passages_ref[p].astype(jnp.float32)
            values = jnp.where(slot_pos < len_ref[p], values, values[0:1])
            filled[p] = values.astype(jnp.bfloat16)
            return carry

        lax.fori_loop(0, passage_count, fill, 0, unroll=8)

    def collect(slot, count):
        live[count] = slot
        return count + (route_ref[slot // per_source, lax.rem(slot, per_source)] >= 0).astype(jnp.int32)

    count = lax.fori_loop(0, slots, collect, jnp.int32(0), unroll=16)
    for spare in range(3):
        live[count + spare] = live[jnp.maximum(count - 1, 0)]
    blank = jnp.zeros((query_len, feature), jnp.bfloat16)

    def one(slot):
        source, query = slot // per_source, lax.rem(slot, per_source)
        base = route_ref[source, query] * cand_count
        tok = q_ref[source, query]
        weights = jnp.concatenate(
            [jnp.concatenate([tok, blank], 1), jnp.concatenate([blank, tok], 1)], 0
        )
        rows = [filled[ids_ref[source, query, base + k]] for k in range(cand_count)]
        left = jnp.concatenate(rows[:groups], 0)
        right = jnp.concatenate(rows[groups:], 0)
        similar = lax.dot_general(
            jnp.concatenate([left, right], 1),
            weights,
            (((1,), (1,)), ((), ())),
            preferred_element_type=jnp.float32,
        )
        for g in range(groups):
            best = jnp.max(similar[g * tokens : (g + 1) * tokens], axis=0, keepdims=True)
            maxima[g, pl.ds(slot, 1), :] = best

    def several(step, carry):
        for turn in range(4):
            one(live[4 * step + turn])
        return carry

    lax.fori_loop(0, (count + 3) // 4, several, 0)

    width = 2 * query_len
    lane = lax.broadcasted_iota(jnp.int32, (width, cand_count), 0)
    column = lax.broadcasted_iota(jnp.int32, (width, cand_count), 1)
    total = jnp.zeros((slots, cand_count), jnp.float32)
    for g in range(groups):
        pick = column == g + groups * (lane >= query_len).astype(jnp.int32)
        pick = pick.astype(jnp.float32).astype(jnp.bfloat16)
        value = maxima[g]
        for _ in range(3):
            part = value.astype(jnp.bfloat16)
            total = total + jnp.dot(part, pick, preferred_element_type=jnp.float32)
            value = value - part.astype(jnp.float32)
    out_ref[...] = (total * (1.0 / query_len)).reshape(out_ref.shape)


def score_slots(route, ids, pass_len, queries, passages, cand_count):
    count, per_source, query_len, feature = queries.shape
    sources = min(count, 16)
    slots = sources * per_source
    return pl.pallas_call(
        score_kernel,
        grid=(count // sources,),
        out_shape=jax.ShapeDtypeStruct((count, per_source, cand_count), jnp.float32),
        in_specs=[
            pl.BlockSpec((sources, per_source), lambda i: (i, 0), memory_space=pltpu.SMEM),
            pl.BlockSpec((sources,) + ids.shape[1:], lambda i: (i, 0, 0), memory_space=pltpu.SMEM),
            pl.BlockSpec(memory_space=pltpu.SMEM),
            pl.BlockSpec((sources, per_source, query_len, feature), lambda i: (i, 0, 0, 0)),
            pl.BlockSpec(passages.shape, lambda i: (0, 0, 0)),
        ],
        out_specs=pl.BlockSpec((sources, per_source, cand_count), lambda i: (i, 0, 0)),
        scratch_shapes=[
            pltpu.VMEM((cand_count // 2, slots, 2 * query_len), jnp.float32),
            pltpu.VMEM(passages.shape, passages.dtype),
            pltpu.SMEM((slots + 3,), jnp.int32),
        ],
        compiler_params=pltpu.CompilerParams(vmem_limit_bytes=48 << 20),
    )(route, ids, pass_len, queries, passages)


def body(queries, passages, pass_len, owners, candidates):
    owner_count = lax.axis_size("shard") * lax.axis_size("sub")
    query_count, route_count, cand_count = candidates.shape
    flat = candidates.reshape(query_count, route_count * cand_count)
    spare = jnp.zeros((7, flat.shape[1]), jnp.int32)
    ids = jnp.concatenate([flat, owners.reshape(1, query_count * route_count), spare], axis=0)
    all_q, all_ids = gather(queries, ids)
    place_in_row = jnp.arange(query_count * route_count, dtype=jnp.int32)
    number = (lax.rem(place_in_row, route_count) + 1).astype(jnp.float32)
    named = jnp.where(all_ids[:, query_count, :] == position(), number[None, :], 0.0)
    fold = place_in_row[:, None] // route_count == jnp.arange(query_count, dtype=jnp.int32)[None, :]
    route = jnp.dot(
        named.astype(jnp.bfloat16), fold.astype(jnp.bfloat16), preferred_element_type=jnp.float32
    ).astype(jnp.int32) - 1
    returned = give_back(score_slots(route, all_ids, pass_len, all_q, passages, cand_count))
    hit = owners[None, :, :] == jnp.arange(owner_count, dtype=jnp.int32)[:, None, None]
    return jnp.sum(jnp.where(hit[..., None], returned[:, :, None, :], 0.0), axis=0)


def solution(mesh):
    in_specs = (
        P(("groups", "shard", "sub"), None, None),
        P(("groups", "shard", "sub"), None, None),
        P(("groups", "shard", "sub")),
        P(("groups", "shard", "sub"), None),
        P(("groups", "shard", "sub"), None, None),
    )
    out_specs = P(("groups", "shard", "sub"), None, None)
    return jax.shard_map(body, mesh=mesh, in_specs=in_specs, out_specs=out_specs, check_vma=False)
```

```python
import jax
import jax.numpy as jnp
from jax import lax
from jax.experimental import pallas as pl
from jax.experimental.pallas import tpu as pltpu
from jax.sharding import PartitionSpec as P

def place(peer):
    subs = lax.axis_size("sub")
    return {"shard": peer // subs, "sub": lax.rem(peer, subs)}


def greet(me, count):
    barrier = pltpu.get_barrier_semaphore()

    def signal(off, carry):
        peer = lax.rem(me + off, count)
        pl.semaphore_signal(barrier, inc=1, device_id=place(peer), device_id_type=pl.DeviceIdType.MESH)
        return carry

    lax.fori_loop(1, count, signal, 0)
    pl.semaphore_wait(barrier, count - 1)


def position():
    return lax.axis_index("shard") * lax.axis_size("sub") + lax.axis_index("sub")


def gather_kernel(q_ref, ids_ref, all_q, all_ids, own_sem, z_send, z_recv, x_send, x_recv, c_send, c_recv):
    depth = lax.axis_size("shard")
    subs = lax.axis_size("sub")
    width = subs // 2
    z, s = lax.axis_index("shard"), lax.axis_index("sub")
    x, core = s // 2, lax.rem(s, 2)
    pairs = ((q_ref, all_q), (ids_ref, all_ids))

    def row(block_z, block_x, block_core):
        return block_z * subs + block_x * 2 + block_core

    def along(step, size, at):
        return lax.rem(at + size + step, size)

    across = {"shard": z, "sub": x * 2 + 1 - core}
    z_peers = [{"shard": along(dz, depth, z), "sub": s} for dz in range(depth)]
    x_peers = [{"shard": z, "sub": along(dx, width, x) * 2 + core} for dx in range(width)]
    mesh_ids = pl.DeviceIdType.MESH

    local = [pltpu.make_async_copy(own, every.at[row(z, x, core)], own_sem.at[i]) for i, (own, every) in enumerate(pairs)]
    for copy in local:
        copy.start()
    barrier = pltpu.get_barrier_semaphore()
    for peer in z_peers[1:] + x_peers[1:] + [across]:
        pl.semaphore_signal(barrier, inc=1, device_id=peer, device_id_type=mesh_ids)
    pl.semaphore_wait(barrier, depth + width - 1)

    def send(block, own, peer, send_sem, recv_sem):
        copies = [
            pltpu.make_async_remote_copy(
                src_ref=mine if own else every.at[block],
                dst_ref=every.at[block],
                send_sem=send_sem(i),
                recv_sem=recv_sem(i),
                device_id=peer,
                device_id_type=mesh_ids,
            )
            for i, (mine, every) in enumerate(pairs)
        ]
        for copy in copies:
            copy.start()
        return copies

    by_z, by_x, by_core = {}, {}, []
    for dz in range(1, depth):
        by_z[dz] = send(
            row(z, x, core), True, z_peers[dz], lambda i: z_send.at[i, dz], lambda i: z_recv.at[i, dz]
        )

    def pass_on(dz):
        block = row(along(-dz, depth, z), x, core)
        for dx in range(1, width):
            by_x[dz, dx] = send(
                block, dz == 0, x_peers[dx], lambda i: x_send.at[i, dz, dx], lambda i: x_recv.at[i, dz, dx]
            )
        by_core.extend(send(block, dz == 0, across, lambda i: c_send.at[i, dz, 0], lambda i: c_recv.at[i, dz, 0]))

    def cross(dz):
        for dx in range(1, width):
            for copy in by_x[dz, dx]:
                copy.wait_recv()
            block = row(along(-dz, depth, z), along(-dx, width, x), core)
            by_core.extend(
                send(block, False, across, lambda i: c_send.at[i, dz, dx], lambda i: c_recv.at[i, dz, dx])
            )

    pass_on(0)
    for dz in range(1, depth):
        for copy in by_z[dz]:
            copy.wait_recv()
        pass_on(dz)
    for dz in range(depth):
        cross(dz)
    for copy in by_core:
        copy.wait()
    for copies in list(by_z.values()) + list(by_x.values()):
        for copy in copies:
            copy.wait_send()
    for copy in local:
        copy.wait()


def gather(queries, ids):
    depth, subs = lax.axis_size("shard"), lax.axis_size("sub")
    count = depth * subs
    sem = pltpu.SemaphoreType.DMA
    return pl.pallas_call(
        gather_kernel,
        out_shape=(
            jax.ShapeDtypeStruct((count,) + queries.shape, queries.dtype),
            jax.ShapeDtypeStruct((count,) + ids.shape, ids.dtype),
        ),
        in_specs=[pl.BlockSpec(memory_space=pl.ANY)] * 2,
        out_specs=[pl.BlockSpec(memory_space=pl.ANY)] * 2,
        scratch_shapes=[sem((2,))] + [sem((2, depth))] * 2 + [sem((2, depth, subs // 2))] * 4,
        compiler_params=pltpu.CompilerParams(collective_id=0, has_side_effects=True),
    )(queries, ids)


def return_kernel(owned_ref, out_ref, own_sem, send, recv):
    count = owned_ref.shape[0]
    me = position()
    local = pltpu.make_async_copy(owned_ref.at[me], out_ref.at[me], own_sem)
    local.start()
    greet(me, count)

    def copy(off):
        peer = lax.rem(me + off, count)
        return pltpu.make_async_remote_copy(
            src_ref=owned_ref.at[peer],
            dst_ref=out_ref.at[me],
            send_sem=send.at[off],
            recv_sem=recv.at[off],
            device_id=place(peer),
            device_id_type=pl.DeviceIdType.MESH,
        )

    def start(off, carry):
        copy(off).start()
        return carry

    def finish(off, carry):
        copy(off).wait()
        return carry

    lax.fori_loop(1, count, start, 0)
    lax.fori_loop(1, count, finish, 0)
    local.wait()


def give_back(owned):
    count = owned.shape[0]
    return pl.pallas_call(
        return_kernel,
        out_shape=jax.ShapeDtypeStruct(owned.shape, owned.dtype),
        in_specs=[pl.BlockSpec(memory_space=pl.ANY)],
        out_specs=pl.BlockSpec(memory_space=pl.ANY),
        scratch_shapes=[pltpu.SemaphoreType.DMA] + [pltpu.SemaphoreType.DMA((count,))] * 2,
        compiler_params=pltpu.CompilerParams(collective_id=1, has_side_effects=True),
    )(owned)


def score_kernel(route_ref, ids_ref, len_ref, q_ref, passages_ref, out_ref, maxima, filled, live):
    sources, per_source, query_len, feature = q_ref.shape
    slots = sources * per_source
    passage_count, tokens, _ = passages_ref.shape
    cand_count = out_ref.shape[-1]
    groups = cand_count // 2
    maxima[...] = jnp.zeros_like(maxima)

    @pl.when(pl.program_id(0) == 0)
    def _():
        slot_pos = lax.broadcasted_iota(jnp.int32, (tokens, feature), 0)

        def fill(p, carry):
            values = passages_ref[p].astype(jnp.float32)
            values = jnp.where(slot_pos < len_ref[p], values, values[0:1])
            filled[p] = values.astype(jnp.bfloat16)
            return carry

        lax.fori_loop(0, passage_count, fill, 0, unroll=8)

    def collect(slot, count):
        live[count] = slot
        return count + (route_ref[slot // per_source, lax.rem(slot, per_source)] >= 0).astype(jnp.int32)

    count = lax.fori_loop(0, slots, collect, jnp.int32(0), unroll=16)
    for spare in range(7):
        live[count + spare] = live[jnp.maximum(count - 1, 0)]
    blank = jnp.zeros((query_len, feature), jnp.bfloat16)

    def one(slot):
        source, query = slot // per_source, lax.rem(slot, per_source)
        base = route_ref[source, query] * cand_count
        tok = q_ref[source, query]
        weights = jnp.concatenate(
            [jnp.concatenate([tok, blank], 1), jnp.concatenate([blank, tok], 1)], 0
        )
        rows = [filled[ids_ref[source, query, base + k]] for k in range(cand_count)]
        left = jnp.concatenate(rows[:groups], 0)
        right = jnp.concatenate(rows[groups:], 0)
        similar = lax.dot_general(
            jnp.concatenate([left, right], 1),
            weights,
            (((1,), (1,)), ((), ())),
            preferred_element_type=jnp.float32,
        )
        for g in range(groups):
            best = jnp.max(similar[g * tokens : (g + 1) * tokens], axis=0, keepdims=True)
            maxima[g, pl.ds(slot, 1), :] = best

    def several(step, carry):
        for turn in range(8):
            one(live[8 * step + turn])
        return carry

    lax.fori_loop(0, (count + 7) // 8, several, 0)

    width = 2 * query_len
    lane = lax.broadcasted_iota(jnp.int32, (width, cand_count), 0)
    column = lax.broadcasted_iota(jnp.int32, (width, cand_count), 1)
    total = jnp.zeros((slots, cand_count), jnp.float32)
    for g in range(groups):
        pick = column == g + groups * (lane >= query_len).astype(jnp.int32)
        pick = pick.astype(jnp.float32).astype(jnp.bfloat16)
        value = maxima[g]
        for _ in range(3):
            part = value.astype(jnp.bfloat16)
            total = total + jnp.dot(part, pick, preferred_element_type=jnp.float32)
            value = value - part.astype(jnp.float32)
    out_ref[...] = (total * (1.0 / query_len)).reshape(out_ref.shape)


def score_slots(route, ids, pass_len, queries, passages, cand_count):
    count, per_source, query_len, feature = queries.shape
    sources = min(count, 16)
    slots = sources * per_source
    return pl.pallas_call(
        score_kernel,
        grid=(count // sources,),
        out_shape=jax.ShapeDtypeStruct((count, per_source, cand_count), jnp.float32),
        in_specs=[
            pl.BlockSpec((sources, per_source), lambda i: (i, 0), memory_space=pltpu.SMEM),
            pl.BlockSpec((sources,) + ids.shape[1:], lambda i: (i, 0, 0), memory_space=pltpu.SMEM),
            pl.BlockSpec(memory_space=pltpu.SMEM),
            pl.BlockSpec((sources, per_source, query_len, feature), lambda i: (i, 0, 0, 0)),
            pl.BlockSpec(passages.shape, lambda i: (0, 0, 0)),
        ],
        out_specs=pl.BlockSpec((sources, per_source, cand_count), lambda i: (i, 0, 0)),
        scratch_shapes=[
            pltpu.VMEM((cand_count // 2, slots, 2 * query_len), jnp.float32),
            pltpu.VMEM(passages.shape, passages.dtype),
            pltpu.SMEM((slots + 7,), jnp.int32),
        ],
        compiler_params=pltpu.CompilerParams(vmem_limit_bytes=48 << 20),
    )(route, ids, pass_len, queries, passages)


def body(queries, passages, pass_len, owners, candidates):
    owner_count = lax.axis_size("shard") * lax.axis_size("sub")
    query_count, route_count, cand_count = candidates.shape
    flat = candidates.reshape(query_count, route_count * cand_count)
    spare = jnp.zeros((7, flat.shape[1]), jnp.int32)
    ids = jnp.concatenate([flat, owners.reshape(1, query_count * route_count), spare], axis=0)
    all_q, all_ids = gather(queries, ids)
    place_in_row = jnp.arange(query_count * route_count, dtype=jnp.int32)
    number = (lax.rem(place_in_row, route_count) + 1).astype(jnp.float32)
    named = jnp.where(all_ids[:, query_count, :] == position(), number[None, :], 0.0)
    fold = place_in_row[:, None] // route_count == jnp.arange(query_count, dtype=jnp.int32)[None, :]
    route = jnp.dot(
        named.astype(jnp.bfloat16), fold.astype(jnp.bfloat16), preferred_element_type=jnp.float32
    ).astype(jnp.int32) - 1
    returned = give_back(score_slots(route, all_ids, pass_len, all_q, passages, cand_count))
    hit = owners[None, :, :] == jnp.arange(owner_count, dtype=jnp.int32)[:, None, None]
    return jnp.sum(jnp.where(hit[..., None], returned[:, :, None, :], 0.0), axis=0)


def solution(mesh):
    in_specs = (
        P(("groups", "shard", "sub"), None, None),
        P(("groups", "shard", "sub"), None, None),
        P(("groups", "shard", "sub")),
        P(("groups", "shard", "sub"), None),
        P(("groups", "shard", "sub"), None, None),
    )
    out_specs = P(("groups", "shard", "sub"), None, None)
    return jax.shard_map(body, mesh=mesh, in_specs=in_specs, out_specs=out_specs, check_vma=False)
```
